32 devices in a mesh: gx: 8 (over z, core), gy: 4 (over y, x).
Axes of the slice: x: 2, y: 2, z: 4, core: 2. Of those that a mesh axis runs over, the one named last changes fastest.
Arguments:
- density: float32 [32, 32, 128], P('gx', 'gy'), may hold values from 0.9 to 1.1
- velocity: float32 [3, 32, 32, 128], P(None, 'gx', 'gy'), may hold values from -0.625 to 0.625
- fluid_mask: int32 [32, 32, 128], P('gx', 'gy'), may hold values 0 or 1
- unit_of_column: int32 [32, 32], P('gx', 'gy'), may hold values from 0 to 31
- radius_base: float32 [256], P(('gx', 'gy')), may hold values from 0.5 to 2
Outputs:
- density_out: float32 [32, 32, 128], P('gx', 'gy')
- velocity_out: float32 [3, 32, 32, 128], P(None, 'gx', 'gy')
- radius_out: float32 [256], P(('gx', 'gy'))
The draws below stay inside these ranges and needn't reach their ends.
All inputs are finite; a program needn't handle non-finite values. No bound on the sum of `fluid_mask` on one device may be relied on, other than what follows from the above.
Results may differ from the reference program's by a relative error of at most 0.0003.
Values sent between devices are 32-bit elements; how exact they have to be, the bound alone decides.
A program may use at most 64 MiB of HBM per device.

```python
import math
import jax
import jax.numpy as jnp

CX = 4
NZ = 128
STEPS = 6
UNIT_DEV = 8
NX = 32
NY = 32
UNITS = 256
N_GY = 4


def set_ends(values, rng, least, largest):
    dims = values.shape
    place = [jax.random.randint(jax.random.fold_in(rng, axis), (), 0, dims[axis]) for axis in range(len(dims))]
    values = values.at[tuple(place)].set(least)
    longest = dims.index(max(dims))
    place[longest] = (place[longest] + 1) % dims[longest]
    return values.at[tuple(place)].set(largest)


def levels(stream_key, shape, split, smallest, largest):
    level = 1.0
    for axis_at, blocks in split:
        steps = jax.random.uniform(jax.random.fold_in(jax.random.fold_in(stream_key, 6), axis_at), (blocks,), jnp.float32, smallest / len(split), largest / len(split))
        level = level * jnp.repeat(jnp.exp(steps), shape[axis_at] // blocks).reshape((-1,) + (1,) * (len(shape) - 1 - axis_at))
    return level


def gaussian(key, extent, spread, most, shards=(), held_as=jnp.bfloat16):
    drawn = spread * jax.random.normal(key, extent, jnp.float32)
    if shards:
        drawn = drawn * levels(key, extent, shards, -0.22, 0.18)
    return jnp.clip(drawn, -most, most).astype(held_as)


def setup_inputs(seed: int = 0) -> dict:
    keys = jax.random.split(jax.random.key(seed), 6)
    return {
        "density": jnp.clip(0.9 + 0.20000005 * jax.random.uniform(keys[0], (NX, NY, NZ), jnp.float32) ** levels(keys[0], (NX, NY, NZ), ((0, 8), (1, 4)), -0.2, 0.2), 0.9, 1.1),
        "velocity": gaussian(keys[1], (3, NX, NY, NZ), 0.04, 0.625, ((1, 8), (2, 4)), jnp.float32),
        "fluid_mask": set_ends((jax.random.randint(keys[2], (NX, NY, NZ), 0, 4) < 3).astype(jnp.int32), jax.random.fold_in(keys[2], 1), 0, 1),
        "unit_of_column": set_ends(jax.random.randint(keys[3], (NX, NY), 0, UNIT_DEV * N_GY), jax.random.fold_in(keys[3], 1), 0, (UNIT_DEV * N_GY) - 1).astype(jnp.int32),
        "radius_base": jnp.clip(jnp.exp(math.log(2.0) - 1.3862944 * jax.random.uniform(keys[4], (UNITS,), jnp.float32) ** levels(keys[4], (UNITS,), ((0, 32),), -0.2, 0.2)), 0.5, 2.0),
    }


LATTICE = ((0, 0, 0), (1, 0, 0), (-1, 0, 0), (0, 1, 0), (0, -1, 0), (0, 0, 1), (0, 0, -1), (1, 1, 0), (-1, -1, 0), (1, -1, 0), (-1, 1, 0), (1, 0, 1), (-1, 0, -1), (1, 0, -1), (-1, 0, 1), (0, 1, 1), (0, -1, -1), (0, 1, -1), (0, -1, 1))
WEIGHTS = (1.0 / 3.0,) + (1.0 / 18.0,) * 6 + (1.0 / 36.0,) * 12
RELAX_RATE = 1.25
DRIVE_SCALE = 0.002


def reverse_of(direction):
    if direction == 0:
        return 0
    return direction + 1 if direction % 2 == 1 else direction - 1


def moments(populations, fluid_share):
    density_now = populations[0]
    momentum = [jnp.zeros_like(density_now) for component in range(3)]
    for direction in range(1, 19):
        density_now = density_now + populations[direction]
        for component in range(3):
            if LATTICE[direction][component] != 0:
                momentum[component] = momentum[component] + LATTICE[direction][component] * populations[direction]
    inverse = 1.0 / (density_now + 1.0 - fluid_share)
    return density_now, [moment * inverse for moment in momentum]


def equilibrium(density_now, velocity_now):
    speed_sq = velocity_now[0] * velocity_now[0] + velocity_now[1] * velocity_now[1] + velocity_now[2] * velocity_now[2]
    balance_terms = []
    for direction in range(19):
        projected = jnp.zeros_like(density_now)
        for component in range(3):
            if LATTICE[direction][component] != 0:
                projected = projected + LATTICE[direction][component] * velocity_now[component]
        balance_terms.append(WEIGHTS[direction] * density_now * (1.0 + 3.0 * projected + 4.5 * projected * projected - 1.5 * speed_sq))
    return jnp.stack(balance_terms)


def collide(populations, density_now, velocity_now, drive_field):
    balance = equilibrium(density_now, velocity_now)
    forcing = jnp.stack([3.0 * WEIGHTS[direction] * LATTICE[direction][2] * drive_field * density_now for direction in range(19)])
    return populations - RELAX_RATE * (populations - balance) + forcing


def stream(padded, mask_padded, collided, fluid_share):
    size_x, size_y, size_z = collided.shape[1:]
    read = []
    for direction in range(19):
        step_x, step_y, step_z = LATTICE[direction]
        source = padded[direction, 1 - step_x:1 - step_x + size_x, 1 - step_y:1 - step_y + size_y, 1 - step_z:1 - step_z + size_z]
        open_site = mask_padded[1 - step_x:1 - step_x + size_x, 1 - step_y:1 - step_y + size_y, 1 - step_z:1 - step_z + size_z]
        read.append(jnp.where(open_site > 0, source, collided[reverse_of(direction)]))
    return jnp.stack(read) * fluid_share


def wall_count(mask_padded, fluid_share):
    size_x, size_y, size_z = fluid_share.shape
    link_total = jnp.zeros_like(fluid_share)
    for direction in range(1, 19):
        step_x, step_y, step_z = LATTICE[direction]
        neighbour = mask_padded[1 + step_x:1 + step_x + size_x, 1 + step_y:1 + step_y + size_y, 1 + step_z:1 + step_z + size_z]
        link_total = link_total + (neighbour == 0).astype(jnp.float32)
    return link_total * fluid_share


def respond(base_radius, shear_sum, link_sum):
    return base_radius * (0.6 + 0.8 * jnp.tanh(100.0 * shear_sum / jnp.maximum(link_sum, 1.0)))


def reference(density, velocity, fluid_mask, unit_of_column, radius_base):
    fluid_share = fluid_mask.astype(jnp.float32)
    mask_padded = jnp.pad(fluid_mask, 1)
    link_count = wall_count(mask_padded, fluid_share)
    populations = equilibrium(density, [velocity[0], velocity[1], velocity[2]]) * fluid_share
    unit_global = ((jnp.arange(NX, dtype=jnp.int32) // CX)[:, None] * (UNIT_DEV * N_GY) + unit_of_column).astype(jnp.int32)
    radius_now = radius_base
    for step_index in range(STEPS):
        density_now, velocity_now = moments(populations, fluid_share)
        speed_sq = velocity_now[0] * velocity_now[0] + velocity_now[1] * velocity_now[1] + velocity_now[2] * velocity_now[2]
        shear_term = jnp.sum(link_count * speed_sq, axis=2)
        link_term = jnp.sum(link_count, axis=2)
        shear_sum = jax.ops.segment_sum(shear_term.reshape(-1), unit_global.reshape(-1), num_segments=UNITS)
        link_sum = jax.ops.segment_sum(link_term.reshape(-1), unit_global.reshape(-1), num_segments=UNITS)
        radius_site = radius_now[unit_global]
        drive_field = (DRIVE_SCALE * radius_site * radius_site)[:, :, None]
        collided = collide(populations, density_now, velocity_now, drive_field)
        padded = jnp.pad(collided, ((0, 0), (1, 1), (1, 1), (1, 1)))
        populations = stream(padded, mask_padded, collided, fluid_share)
        radius_now = respond(radius_base, shear_sum, link_sum)
    density_now, velocity_now = moments(populations, fluid_share)
    return density_now, jnp.stack(velocity_now), radius_now
```

```python
import functools

import jax
import jax.numpy as jnp
from jax import lax
from jax.experimental import pallas as pl
from jax.experimental.pallas import tpu as pltpu
from jax.sharding import PartitionSpec as P

STEPS = 6

LATTICE = (
    (0, 0, 0),
    (1, 0, 0),
    (-1, 0, 0),
    (0, 1, 0),
    (0, -1, 0),
    (0, 0, 1),
    (0, 0, -1),
    (1, 1, 0),
    (-1, -1, 0),
    (1, -1, 0),
    (-1, 1, 0),
    (1, 0, 1),
    (-1, 0, -1),
    (1, 0, -1),
    (-1, 0, 1),
    (0, 1, 1),
    (0, -1, -1),
    (0, 1, -1),
    (0, -1, 1),
)
WEIGHTS = (1.0 / 3.0,) + (1.0 / 18.0,) * 6 + (1.0 / 36.0,) * 12
RELAX_RATE = 1.25
DRIVE_SCALE = 0.002
MESH = pl.DeviceIdType.MESH

X_DIRS = {s: [i for i, c in enumerate(LATTICE) if c[0] == s] for s in (1, -1)}
Y_DIRS = {s: [i for i, c in enumerate(LATTICE) if c[1] == s] for s in (1, -1)}
CORNERS = [i for i, c in enumerate(LATTICE) if c[0] and c[1]]


def reverse_of(direction):
    if direction == 0:
        return 0
    return direction + 1 if direction % 2 == 1 else direction - 1


def kernel(
    n_gx,
    n_gy,
    density_ref,
    velocity_ref,
    mask_ref,
    unit_ref,
    base_ref,
    density_out,
    velocity_out,
    radius_out,
    open_ref,
    links_ref,
    onehot_ref,
    row_ref,
    post_ref,
    rolled_ref,
    x_send,
    y_send,
    c_send,
    s_send,
    x_recv,
    y_recv,
    c_recv,
    s_recv,
    send_sem,
    recv_sem,
):
    size_x, size_y, size_z = density_ref.shape
    units_own = base_ref.shape[0]
    lanes = s_send.shape[-1]
    gx = lax.axis_index("gx")
    gy = lax.axis_index("gy")
    f32 = jnp.float32

    def inside(dx, dy):
        ok = None
        for pos, step, count in ((gx, dx, n_gx), (gy, dy, n_gy)):
            if step == 0:
                continue
            here = pos + step < count if step > 0 else pos + step >= 0
            ok = here if ok is None else jnp.logical_and(ok, here)
        return ok

    def messages(par):
        out = []
        for k, s in enumerate((1, -1)):
            out.append((s, 0, x_send.at[k], x_recv.at[par, k]))
        for k, s in enumerate((1, -1)):
            out.append((0, s, y_send.at[k], y_recv.at[par, k]))
        for k, i in enumerate(CORNERS):
            out.append((LATTICE[i][0], LATTICE[i][1], c_send.at[k], c_recv.at[par, k]))
        return [m + (n,) for n, m in enumerate(out)]

    def remote(par, dx, dy, src, dst, n):
        return pltpu.make_async_remote_copy(
            src_ref=src,
            dst_ref=dst,
            send_sem=send_sem.at[n],
            recv_sem=recv_sem.at[par, n],
            device_id=(gx + dx, gy + dy),
            device_id_type=MESH,
        )

    def row_copy(par, j, slot):
        return pltpu.make_async_remote_copy(
            src_ref=s_send,
            dst_ref=s_recv.at[par, slot],
            send_sem=send_sem.at[7 + j],
            recv_sem=recv_sem.at[par, 7 + j],
            device_id=(gx, lax.rem(gy + j, n_gy)),
            device_id_type=MESH,
        )

    def send_all(par):
        for j in range(1, n_gy):
            row_copy(par, j, gy).start()
        order = messages(par)
        for dx, dy, src, dst, n in order[4:] + order[:4]:
            pl.when(inside(dx, dy))(lambda: remote(par, dx, dy, src, dst, n).start())

    def wait_all(par):
        for j in range(1, n_gy):
            row_copy(par, j, lax.rem(gy - j + n_gy, n_gy)).wait()
        for dx, dy, src, dst, n in messages(par):
            pl.when(inside(-dx, -dy))(
                lambda: remote(par, dx, dy, src, dst, n).wait_recv()
            )
        for dx, dy, src, dst, n in messages(par):
            pl.when(inside(dx, dy))(lambda: remote(par, dx, dy, src, dst, n).wait_send())

    sublane = lax.broadcasted_iota(jnp.int32, (size_y, size_z), 0)
    lane = lax.broadcasted_iota(jnp.int32, (size_y, size_z), 1)

    def put(par, i, x, value):
        sx, sy, sz = LATTICE[i]
        if sz:
            value = pltpu.roll(value, sz % size_z, 1)
        if sy:
            value = pltpu.roll(value, sy % size_y, 0)
        rolled_ref[par, i, x] = value
        edge = size_x - 1 if sx > 0 else 0
        if sx and x == edge:
            side = 0 if sx > 0 else 1
            x_send[side, X_DIRS[sx].index(i)] = value
        if sy:
            side, row = (0, 0) if sy > 0 else (1, size_y - 1)
            line = value[row : row + 1, :]
            at = Y_DIRS[sy].index(i) * size_x + x
            y_send[side, at : at + 1, :] = line
            if sx and x == edge:
                c_send[CORNERS.index(i)] = line

    def pull(old, rx, i, x):
        sx, sy, sz = LATTICE[i]
        at = x - sx
        crossed = at < 0 or at >= size_x
        if crossed:
            value = x_recv[rx, 0 if sx > 0 else 1, X_DIRS[sx].index(i)]
        else:
            value = rolled_ref[old, i, at]
        if sy:
            side, row = (0, 0) if sy > 0 else (1, size_y - 1)
            if crossed:
                line = c_recv[rx, CORNERS.index(i)]
            else:
                slot = Y_DIRS[sy].index(i) * size_x + at
                line = y_recv[rx, side, slot : slot + 1, :]
            value = jnp.where(sublane == row, line, value)
        return value

    def total_rows(par):
        total = s_send[...]
        for j in range(n_gy):
            total = total + s_recv[par, j]
        return total

    def drive_tiles(radius_row):
        drive_row = (DRIVE_SCALE * radius_row) * radius_row
        return [
            jnp.sum(onehot_ref[x] * drive_row, axis=1, keepdims=True) for x in range(size_x)
        ]

    def relax(par, x, pops, rho, vel, drive):
        keep = 0.0 if pops is None else 1.0 - RELAX_RATE
        rate = 1.0 if pops is None else RELAX_RATE
        ux, uy, uz = vel
        speed = ux * ux + uy * uy + uz * uz
        rel = rate * rho
        level = rel - (1.5 * speed) * rel
        push = [(3.0 * rel) * u for u in vel]
        push[2] = push[2] + (3.0 * drive) * rho
        posts = [None] * 19
        rest = WEIGHTS[0] * level
        posts[0] = rest if pops is None else keep * pops[0] + rest
        for i in range(1, 19, 2):
            step = LATTICE[i]
            proj = None
            odd = None
            for comp in range(3):
                if step[comp] == 0:
                    continue
                if proj is None:
                    proj, odd = vel[comp], push[comp]
                elif step[comp] > 0:
                    proj, odd = proj + vel[comp], odd + push[comp]
                else:
                    proj, odd = proj - vel[comp], odd - push[comp]
            even = level + (4.5 * rel) * (proj * proj)
            for k, value in ((i, even + odd), (i + 1, even - odd)):
                value = WEIGHTS[i] * value
                posts[k] = value if pops is None else keep * pops[k] + value
        for i in range(19):
            post_ref[par, i, x] = posts[i]
            if i:
                put(par, i, x, posts[i])
        return speed

    def spread(x, speed):
        term = jnp.sum(links_ref[x] * speed, axis=1, keepdims=True)
        return onehot_ref[x] * term

    def gathered(old, rx, x, fl):
        pops = [post_ref[old, 0, x]]
        for i in range(1, 19):
            moved = pull(old, rx, i, x)
            pops.append(
                jnp.where(open_ref[i, x] > 0.0, moved, post_ref[old, reverse_of(i), x])
            )
        rho = pops[0]
        for i in range(1, 19):
            rho = rho + pops[i]
        momentum = []
        for comp in range(3):
            up = functools.reduce(
                lambda a, b: a + b, [pops[i] for i in range(19) if LATTICE[i][comp] == 1]
            )
            down = functools.reduce(
                lambda a, b: a + b, [pops[i] for i in range(19) if LATTICE[i][comp] == -1]
            )
            momentum.append(up - down)
        inverse = 1.0 / (rho + 1.0 - fl)
        return pops, rho, [m * inverse for m in momentum]

    def respond(par):
        total = total_rows(par)
        return row_ref[0:1, :] * (
            0.6
            + 0.8 * jnp.tanh(100.0 * total[0:1, :] / jnp.maximum(total[1:2, :], 1.0))
        )

    x_recv[...] = jnp.zeros_like(x_recv)
    y_recv[...] = jnp.zeros_like(y_recv)
    c_recv[...] = jnp.zeros_like(c_recv)
    s_recv[...] = jnp.zeros_like(s_recv)

    barrier = pltpu.get_barrier_semaphore()
    expected = jnp.int32(n_gy - 1)
    for j in range(1, n_gy):
        pl.semaphore_signal(
            barrier, inc=1, device_id=(gx, lax.rem(gy + j, n_gy)), device_id_type=MESH
        )
    for dx in (-1, 1):
        for dy in (-1, 0, 1):
            ok = inside(dx, dy)
            pl.when(ok)(
                lambda: pl.semaphore_signal(
                    barrier, inc=1, device_id=(gx + dx, gy + dy), device_id_type=MESH
                )
            )
            expected = expected + ok.astype(jnp.int32)

    shares = [mask_ref[x].astype(f32) for x in range(size_x)]
    for x in range(size_x):
        for i in range(1, 19):
            put(0, i, x, shares[x])
    wide = lax.broadcasted_iota(jnp.int32, (1, lanes), 1)
    own_row = jnp.zeros((1, lanes), f32)
    for j in range(units_own):
        own_row = jnp.where(wide == gy * units_own + j, base_ref[j], own_row)
    s_send[0:1, :] = own_row
    s_send[1:2, :] = jnp.zeros((1, lanes), f32)
    pl.semaphore_wait(barrier, expected)
    send_all(0)

    wide_y = lax.broadcasted_iota(jnp.int32, (size_y, lanes), 1)
    eye = lax.broadcasted_iota(jnp.int32, (size_y, size_y), 0) == lax.broadcasted_iota(
        jnp.int32, (size_y, size_y), 1
    )
    for x in range(size_x):
        names = jnp.broadcast_to(unit_ref[x : x + 1, :].astype(f32), (size_y, size_y))
        names = jnp.sum(jnp.where(eye, names, 0.0), axis=1, keepdims=True)
        onehot_ref[x] = jnp.where(wide_y.astype(f32) == names, 1.0, 0.0)

    wait_all(0)
    link_part = jnp.zeros((size_y, lanes), f32)
    for x in range(size_x):
        count = jnp.full((size_y, size_z), 18.0, f32)
        for i in range(1, 19):
            sz = LATTICE[i][2]
            value = pull(0, 0, i, x)
            if sz:
                value = jnp.where(lane == (0 if sz > 0 else size_z - 1), 0.0, value)
            value = value * shares[x]
            open_ref[i, x] = value
            count = count - value
        links_ref[x] = count * shares[x]
        link_part = link_part + spread(x, 1.0)
    row_ref[...] = total_rows(0)

    drives = drive_tiles(row_ref[0:1, :])
    part = jnp.zeros((size_y, lanes), f32)
    for x in range(size_x):
        rho = density_ref[x] * shares[x]
        vel = [velocity_ref[c, x] * shares[x] for c in range(3)]
        part = part + spread(x, relax(1, x, None, rho, vel, drives[x]))
    s_send[0:1, :] = jnp.sum(part, axis=0, keepdims=True)
    s_send[1:2, :] = jnp.sum(link_part, axis=0, keepdims=True)
    send_all(1)

    def step(r, carry):
        old = lax.rem(r, 2)
        new = 1 - old
        wait_all(old)
        drives = drive_tiles(respond(old))
        part = jnp.zeros((size_y, lanes), f32)
        for x in range(size_x):
            fl = mask_ref[x].astype(f32)
            pops, rho, vel = gathered(old, old, x, fl)
            part = part + spread(x, relax(new, x, pops, rho, vel, drives[x]))
        s_send[0:1, :] = jnp.sum(part, axis=0, keepdims=True)
        send_all(new)
        return carry

    lax.fori_loop(1, STEPS, step, 0)

    last = STEPS % 2
    wait_all(last)
    radius = respond(last)
    radius = pltpu.roll(
        jnp.broadcast_to(radius, (8, lanes)), lax.rem(lanes - gy * units_own, lanes), 1
    )
    radius_out[...] = radius[0:1, 0:units_own]
    for x in range(size_x):
        fl = mask_ref[x].astype(f32)
        pops, rho, vel = gathered(last, last, x, fl)
        density_out[x] = rho
        for comp in range(3):
            velocity_out[comp, x] = vel[comp]


def per_device(n_gx, n_gy, density, velocity, fluid_mask, unit_of_column, radius_base):
    size_x, size_y, size_z = density.shape
    units_own = radius_base.shape[0]
    lanes = -(-units_own * n_gy // 128) * 128
    f32 = jnp.float32
    tile = (size_x, size_y, size_z)
    copies = 7 + n_gy + 1
    vmem = pl.BlockSpec(memory_space=pltpu.VMEM)
    smem = pl.BlockSpec(memory_space=pltpu.SMEM)
    rho, vel, radius = pl.pallas_call(
        functools.partial(kernel, n_gx, n_gy),
        out_shape=(
            jax.ShapeDtypeStruct(density.shape, f32),
            jax.ShapeDtypeStruct(velocity.shape, f32),
            jax.ShapeDtypeStruct((1, units_own), f32),
        ),
        in_specs=[vmem, vmem, vmem, vmem, smem],
        out_specs=(vmem, vmem, vmem),
        scratch_shapes=[
            pltpu.VMEM((19,) + tile, f32),
            pltpu.VMEM(tile, f32),
            pltpu.VMEM((size_x, size_y, lanes), f32),
            pltpu.VMEM((2, lanes), f32),
            pltpu.VMEM((2, 19) + tile, f32),
            pltpu.VMEM((2, 19) + tile, f32),
            pltpu.VMEM((2, 5, size_y, size_z), f32),
            pltpu.VMEM((2, 5 * size_x, size_z), f32),
            pltpu.VMEM((4, 1, size_z), f32),
            pltpu.VMEM((2, lanes), f32),
            pltpu.VMEM((2, 2, 5, size_y, size_z), f32),
            pltpu.VMEM((2, 2, 5 * size_x, size_z), f32),
            pltpu.VMEM((2, 4, 1, size_z), f32),
            pltpu.VMEM((2, n_gy, 2, lanes), f32),
            pltpu.SemaphoreType.DMA((copies,)),
            pltpu.SemaphoreType.DMA((2, copies)),
        ],
        compiler_params=pltpu.CompilerParams(collective_id=0, has_side_effects=True),
    )(density, velocity, fluid_mask, unit_of_column, radius_base)
    return rho, vel, radius.reshape(units_own)


def solution(mesh):
    return jax.shard_map(
        functools.partial(per_device, mesh.shape["gx"], mesh.shape["gy"]),
        mesh=mesh,
        in_specs=(
            P("gx", "gy", None),
            P(None, "gx", "gy", None),
            P("gx", "gy", None),
            P("gx", "gy"),
            P(("gx", "gy")),
        ),
        out_specs=(P("gx", "gy", None), P(None, "gx", "gy", None), P(("gx", "gy"))),
        check_vma=False,
    )
```

```python
import functools

import jax
import jax.numpy as jnp
from jax import lax
from jax.experimental import pallas as pl
from jax.experimental.pallas import tpu as pltpu
from jax.sharding import PartitionSpec as P

STEPS = 6

LATTICE = (
    (0, 0, 0),
    (1, 0, 0),
    (-1, 0, 0),
    (0, 1, 0),
    (0, -1, 0),
    (0, 0, 1),
    (0, 0, -1),
    (1, 1, 0),
    (-1, -1, 0),
    (1, -1, 0),
    (-1, 1, 0),
    (1, 0, 1),
    (-1, 0, -1),
    (1, 0, -1),
    (-1, 0, 1),
    (0, 1, 1),
    (0, -1, -1),
    (0, 1, -1),
    (0, -1, 1),
)
WEIGHTS = (1.0 / 3.0,) + (1.0 / 18.0,) * 6 + (1.0 / 36.0,) * 12
RELAX_RATE = 1.25
DRIVE_SCALE = 0.002
MESH = pl.DeviceIdType.MESH

X_DIRS = {s: [i for i, c in enumerate(LATTICE) if c[0] == s] for s in (1, -1)}
Y_DIRS = {s: [i for i, c in enumerate(LATTICE) if c[1] == s] for s in (1, -1)}
CORNERS = [i for i, c in enumerate(LATTICE) if c[0] and c[1]]


def reverse_of(direction):
    if direction == 0:
        return 0
    return direction + 1 if direction % 2 == 1 else direction - 1


def kernel(
    n_gx,
    n_gy,
    density_ref,
    velocity_ref,
    mask_ref,
    unit_ref,
    base_ref,
    density_out,
    velocity_out,
    radius_out,
    open_ref,
    links_ref,
    onehot_ref,
    row_ref,
    post_ref,
    rolled_ref,
    x_send,
    y_send,
    c_send,
    s_send,
    x_recv,
    y_recv,
    c_recv,
    s_recv,
    send_sem,
    recv_sem,
):
    size_x, size_y, size_z = density_ref.shape
    units_own = base_ref.shape[0]
    lanes = s_send.shape[-1]
    gx = lax.axis_index("gx")
    gy = lax.axis_index("gy")
    f32 = jnp.float32

    def inside(dx, dy):
        ok = None
        for pos, step, count in ((gx, dx, n_gx), (gy, dy, n_gy)):
            if step == 0:
                continue
            here = pos + step < count if step > 0 else pos + step >= 0
            ok = here if ok is None else jnp.logical_and(ok, here)
        return ok

    def messages(par):
        out = []
        for k, s in enumerate((1, -1)):
            out.append((s, 0, x_send.at[par, k], x_recv.at[par, k]))
        for k, s in enumerate((1, -1)):
            out.append((0, s, y_send.at[par, k], y_recv.at[par, k]))
        for k, i in enumerate(CORNERS):
            out.append((LATTICE[i][0], LATTICE[i][1], c_send.at[par, k], c_recv.at[par, k]))
        return [m + (n,) for n, m in enumerate(out)]

    def remote(par, dx, dy, src, dst, n):
        return pltpu.make_async_remote_copy(
            src_ref=src,
            dst_ref=dst,
            send_sem=send_sem.at[par, n],
            recv_sem=recv_sem.at[par, n],
            device_id=(gx + dx, gy + dy),
            device_id_type=MESH,
        )

    def row_copy(par, j, slot):
        return pltpu.make_async_remote_copy(
            src_ref=s_send.at[par],
            dst_ref=s_recv.at[par, slot],
            send_sem=send_sem.at[par, 7 + j],
            recv_sem=recv_sem.at[par, 7 + j],
            device_id=(gx, lax.rem(gy + j, n_gy)),
            device_id_type=MESH,
        )

    def send_all(par):
        for j in range(1, n_gy):
            row_copy(par, j, gy).start()
        order = messages(par)
        for dx, dy, src, dst, n in order[4:] + order[:4]:
            pl.when(inside(dx, dy))(lambda: remote(par, dx, dy, src, dst, n).start())

    def wait_all(par):
        for j in range(1, n_gy):
            row_copy(par, j, lax.rem(gy - j + n_gy, n_gy)).wait_recv()
        for dx, dy, src, dst, n in messages(par):
            pl.when(inside(-dx, -dy))(
                lambda: remote(par, dx, dy, src, dst, n).wait_recv()
            )

    def wait_sent(par):
        for j in range(1, n_gy):
            row_copy(par, j, gy).wait_send()
        for dx, dy, src, dst, n in messages(par):
            pl.when(inside(dx, dy))(lambda: remote(par, dx, dy, src, dst, n).wait_send())

    sublane = lax.broadcasted_iota(jnp.int32, (size_y, size_z), 0)
    lane = lax.broadcasted_iota(jnp.int32, (size_y, size_z), 1)

    def put(par, i, x, value):
        sx, sy, sz = LATTICE[i]
        if sz:
            value = pltpu.roll(value, sz % size_z, 1)
        if sy:
            value = pltpu.roll(value, sy % size_y, 0)
        rolled_ref[par, i, x] = value
        edge = size_x - 1 if sx > 0 else 0
        if sx and x == edge:
            side = 0 if sx > 0 else 1
            x_send[par, side, X_DIRS[sx].index(i)] = value
        if sy:
            side, row = (0, 0) if sy > 0 else (1, size_y - 1)
            line = value[row : row + 1, :]
            at = Y_DIRS[sy].index(i) * size_x + x
            y_send[par, side, at : at + 1, :] = line
            if sx and x == edge:
                c_send[par, CORNERS.index(i)] = line

    def pull(old, rx, i, x):
        sx, sy, sz = LATTICE[i]
        at = x - sx
        crossed = at < 0 or at >= size_x
        if crossed:
            value = x_recv[rx, 0 if sx > 0 else 1, X_DIRS[sx].index(i)]
        else:
            value = rolled_ref[old, i, at]
        if sy:
            side, row = (0, 0) if sy > 0 else (1, size_y - 1)
            if crossed:
                line = c_recv[rx, CORNERS.index(i)]
            else:
                slot = Y_DIRS[sy].index(i) * size_x + at
                line = y_recv[rx, side, slot : slot + 1, :]
            value = jnp.where(sublane == row, line, value)
        return value

    def total_rows(par):
        total = s_send[par]
        for j in range(n_gy):
            total = total + s_recv[par, j]
        return total

    def drive_tiles(radius_row):
        drive_row = (DRIVE_SCALE * radius_row) * radius_row
        return [
            jnp.sum(onehot_ref[x] * drive_row, axis=1, keepdims=True) for x in range(size_x)
        ]

    def relax(par, x, pops, rho, vel, drive):
        keep = 0.0 if pops is None else 1.0 - RELAX_RATE
        rate = 1.0 if pops is None else RELAX_RATE
        ux, uy, uz = vel
        speed = ux * ux + uy * uy + uz * uz
        rel = rate * rho
        level = rel - (1.5 * speed) * rel
        push = [(3.0 * rel) * u for u in vel]
        push[2] = push[2] + (3.0 * drive) * rho
        posts = [None] * 19
        rest = WEIGHTS[0] * level
        posts[0] = rest if pops is None else keep * pops[0] + rest
        for i in range(1, 19, 2):
            step = LATTICE[i]
            proj = None
            odd = None
            for comp in range(3):
                if step[comp] == 0:
                    continue
                if proj is None:
                    proj, odd = vel[comp], push[comp]
                elif step[comp] > 0:
                    proj, odd = proj + vel[comp], odd + push[comp]
                else:
                    proj, odd = proj - vel[comp], odd - push[comp]
            even = level + (4.5 * rel) * (proj * proj)
            for k, value in ((i, even + odd), (i + 1, even - odd)):
                value = WEIGHTS[i] * value
                posts[k] = value if pops is None else keep * pops[k] + value
        for i in range(19):
            post_ref[par, i, x] = posts[i]
            if i:
                put(par, i, x, posts[i])
        return speed

    def spread(x, speed):
        term = jnp.sum(links_ref[x] * speed, axis=1, keepdims=True)
        return onehot_ref[x] * term

    def gathered(old, rx, x, fl):
        pops = [post_ref[old, 0, x]]
        for i in range(1, 19):
            moved = pull(old, rx, i, x)
            pops.append(
                jnp.where(open_ref[i, x] > 0.0, moved, post_ref[old, reverse_of(i), x])
            )
        rho = pops[0]
        for i in range(1, 19):
            rho = rho + pops[i]
        momentum = []
        for comp in range(3):
            up = functools.reduce(
                lambda a, b: a + b, [pops[i] for i in range(19) if LATTICE[i][comp] == 1]
            )
            down = functools.reduce(
                lambda a, b: a + b, [pops[i] for i in range(19) if LATTICE[i][comp] == -1]
            )
            momentum.append(up - down)
        inverse = 1.0 / (rho + 1.0 - fl)
        return pops, rho, [m * inverse for m in momentum]

    def respond(par):
        total = total_rows(par)
        return row_ref[0:1, :] * (
            0.6
            + 0.8 * jnp.tanh(100.0 * total[0:1, :] / jnp.maximum(total[1:2, :], 1.0))
        )

    x_recv[...] = jnp.zeros_like(x_recv)
    y_recv[...] = jnp.zeros_like(y_recv)
    c_recv[...] = jnp.zeros_like(c_recv)
    s_recv[...] = jnp.zeros_like(s_recv)

    barrier = pltpu.get_barrier_semaphore()
    expected = jnp.int32(n_gy - 1)
    for j in range(1, n_gy):
        pl.semaphore_signal(
            barrier, inc=1, device_id=(gx, lax.rem(gy + j, n_gy)), device_id_type=MESH
        )
    for dx in (-1, 1):
        for dy in (-1, 0, 1):
            ok = inside(dx, dy)
            pl.when(ok)(
                lambda: pl.semaphore_signal(
                    barrier, inc=1, device_id=(gx + dx, gy + dy), device_id_type=MESH
                )
            )
            expected = expected + ok.astype(jnp.int32)

    shares = [mask_ref[x].astype(f32) for x in range(size_x)]
    for x in range(size_x):
        for i in range(1, 19):
            put(0, i, x, shares[x])
    wide = lax.broadcasted_iota(jnp.int32, (1, lanes), 1)
    own_row = jnp.zeros((1, lanes), f32)
    for j in range(units_own):
        own_row = jnp.where(wide == gy * units_own + j, base_ref[j], own_row)
    s_send[0, 0:1, :] = own_row
    s_send[0, 1:2, :] = jnp.zeros((1, lanes), f32)
    pl.semaphore_wait(barrier, expected)
    send_all(0)

    wide_y = lax.broadcasted_iota(jnp.int32, (size_y, lanes), 1)
    eye = lax.broadcasted_iota(jnp.int32, (size_y, size_y), 0) == lax.broadcasted_iota(
        jnp.int32, (size_y, size_y), 1
    )
    for x in range(size_x):
        names = jnp.broadcast_to(unit_ref[x : x + 1, :].astype(f32), (size_y, size_y))
        names = jnp.sum(jnp.where(eye, names, 0.0), axis=1, keepdims=True)
        onehot_ref[x] = jnp.where(wide_y.astype(f32) == names, 1.0, 0.0)

    wait_all(0)
    link_part = jnp.zeros((size_y, lanes), f32)
    for x in range(size_x):
        count = jnp.full((size_y, size_z), 18.0, f32)
        for i in range(1, 19):
            sz = LATTICE[i][2]
            value = pull(0, 0, i, x)
            if sz:
                value = jnp.where(lane == (0 if sz > 0 else size_z - 1), 0.0, value)
            value = value * shares[x]
            open_ref[i, x] = value
            count = count - value
        links_ref[x] = count * shares[x]
        link_part = link_part + spread(x, 1.0)
    row_ref[...] = total_rows(0)

    drives = drive_tiles(row_ref[0:1, :])
    part = jnp.zeros((size_y, lanes), f32)
    for x in range(size_x):
        rho = density_ref[x] * shares[x]
        vel = [velocity_ref[c, x] * shares[x] for c in range(3)]
        part = part + spread(x, relax(1, x, None, rho, vel, drives[x]))
    s_send[1, 0:1, :] = jnp.sum(part, axis=0, keepdims=True)
    link_row = jnp.sum(link_part, axis=0, keepdims=True)
    s_send[1, 1:2, :] = link_row
    send_all(1)
    wait_sent(0)
    s_send[0, 1:2, :] = link_row

    def step(r, carry):
        old = lax.rem(r, 2)
        new = 1 - old
        wait_all(old)
        drives = drive_tiles(respond(old))
        part = jnp.zeros((size_y, lanes), f32)
        for x in range(size_x):
            fl = mask_ref[x].astype(f32)
            pops, rho, vel = gathered(old, old, x, fl)
            part = part + spread(x, relax(new, x, pops, rho, vel, drives[x]))
        s_send[new, 0:1, :] = jnp.sum(part, axis=0, keepdims=True)
        send_all(new)
        wait_sent(old)
        return carry

    lax.fori_loop(1, STEPS, step, 0)

    last = STEPS % 2
    wait_all(last)
    wait_sent(last)
    radius = respond(last)
    radius = pltpu.roll(
        jnp.broadcast_to(radius, (8, lanes)), lax.rem(lanes - gy * units_own, lanes), 1
    )
    radius_out[...] = radius[0:1, 0:units_own]
    for x in range(size_x):
        fl = mask_ref[x].astype(f32)
        pops, rho, vel = gathered(last, last, x, fl)
        density_out[x] = rho
        for comp in range(3):
            velocity_out[comp, x] = vel[comp]


def hand_over(rho, vel, radius, rho_out, vel_out, radius_out):
    rho_out[...] = rho[...]
    vel_out[...] = vel[...]
    radius_out[...] = radius[...]


def per_device(n_gx, n_gy, density, velocity, fluid_mask, unit_of_column, radius_base):
    size_x, size_y, size_z = density.shape
    units_own = radius_base.shape[0]
    lanes = -(-units_own * n_gy // 128) * 128
    f32 = jnp.float32
    tile = (size_x, size_y, size_z)
    copies = 7 + n_gy + 1
    vmem = pl.BlockSpec(memory_space=pltpu.VMEM)
    smem = pl.BlockSpec(memory_space=pltpu.SMEM)
    rho, vel, radius = pl.pallas_call(
        functools.partial(kernel, n_gx, n_gy),
        out_shape=(
            jax.ShapeDtypeStruct(density.shape, f32),
            jax.ShapeDtypeStruct(velocity.shape, f32),
            jax.ShapeDtypeStruct((1, units_own), f32),
        ),
        in_specs=[vmem, vmem, vmem, vmem, smem],
        out_specs=(vmem, vmem, vmem),
        scratch_shapes=[
            pltpu.VMEM((19,) + tile, f32),
            pltpu.VMEM(tile, f32),
            pltpu.VMEM((size_x, size_y, lanes), f32),
            pltpu.VMEM((2, lanes), f32),
            pltpu.VMEM((2, 19) + tile, f32),
            pltpu.VMEM((2, 19) + tile, f32),
            pltpu.VMEM((2, 2, 5, size_y, size_z), f32),
            pltpu.VMEM((2, 2, 5 * size_x, size_z), f32),
            pltpu.VMEM((2, 4, 1, size_z), f32),
            pltpu.VMEM((2, 2, lanes), f32),
            pltpu.VMEM((2, 2, 5, size_y, size_z), f32),
            pltpu.VMEM((2, 2, 5 * size_x, size_z), f32),
            pltpu.VMEM((2, 4, 1, size_z), f32),
            pltpu.VMEM((2, n_gy, 2, lanes), f32),
            pltpu.SemaphoreType.DMA((2, copies)),
            pltpu.SemaphoreType.DMA((2, copies)),
        ],
        compiler_params=pltpu.CompilerParams(collective_id=0, has_side_effects=True),
    )(density, velocity, fluid_mask, unit_of_column, radius_base)
    rho, vel, radius = pl.pallas_call(
        hand_over,
        out_shape=(
            jax.ShapeDtypeStruct(density.shape, f32),
            jax.ShapeDtypeStruct(velocity.shape, f32),
            jax.ShapeDtypeStruct((1, units_own), f32),
        ),
        in_specs=[vmem, vmem, vmem],
        out_specs=(vmem, vmem, vmem),
    )(rho, vel, radius)
    return rho, vel, radius.reshape(units_own)


def solution(mesh):
    return jax.shard_map(
        functools.partial(per_device, mesh.shape["gx"], mesh.shape["gy"]),
        mesh=mesh,
        in_specs=(
            P("gx", "gy", None),
            P(None, "gx", "gy", None),
            P("gx", "gy", None),
            P("gx", "gy"),
            P(("gx", "gy")),
        ),
        out_specs=(P("gx", "gy", None), P(None, "gx", "gy", None), P(("gx", "gy"))),
        check_vma=False,
    )
```

```python
import functools

import jax
import jax.numpy as jnp
from jax import lax
from jax.experimental import pallas as pl
from jax.experimental.pallas import tpu as pltpu
from jax.sharding import PartitionSpec as P

STEPS = 6

LATTICE = (
    (0, 0, 0),
    (1, 0, 0),
    (-1, 0, 0),
    (0, 1, 0),
    (0, -1, 0),
    (0, 0, 1),
    (0, 0, -1),
    (1, 1, 0),
    (-1, -1, 0),
    (1, -1, 0),
    (-1, 1, 0),
    (1, 0, 1),
    (-1, 0, -1),
    (1, 0, -1),
    (-1, 0, 1),
    (0, 1, 1),
    (0, -1, -1),
    (0, 1, -1),
    (0, -1, 1),
)
WEIGHTS = (1.0 / 3.0,) + (1.0 / 18.0,) * 6 + (1.0 / 36.0,) * 12
RELAX_RATE = 1.25
DRIVE_SCALE = 0.002
MESH = pl.DeviceIdType.MESH

X_DIRS = {s: [i for i, c in enumerate(LATTICE) if c[0] == s] for s in (1, -1)}
Y_DIRS = {s: [i for i, c in enumerate(LATTICE) if c[1] == s] for s in (1, -1)}
CORNERS = [i for i, c in enumerate(LATTICE) if c[0] and c[1]]


def reverse_of(direction):
    if direction == 0:
        return 0
    return direction + 1 if direction % 2 == 1 else direction - 1


def kernel(
    n_gx,
    n_gy,
    density_ref,
    velocity_ref,
    mask_ref,
    unit_ref,
    base_ref,
    density_out,
    velocity_out,
    radius_out,
    open_ref,
    links_ref,
    onehot_ref,
    row_ref,
    post_ref,
    rolled_ref,
    x_send,
    y_send,
    c_send,
    s_send,
    x_recv,
    y_recv,
    c_recv,
    s_recv,
    send_sem,
    recv_sem,
):
    size_x, size_y, size_z = density_ref.shape
    units_own = base_ref.shape[0]
    lanes = s_send.shape[-1]
    gx = lax.axis_index("gx")
    gy = lax.axis_index("gy")
    f32 = jnp.float32

    def inside(dx, dy):
        ok = None
        for pos, step, count in ((gx, dx, n_gx), (gy, dy, n_gy)):
            if step == 0:
                continue
            here = pos + step < count if step > 0 else pos + step >= 0
            ok = here if ok is None else jnp.logical_and(ok, here)
        return ok

    def messages(par):
        out = []
        for k, s in enumerate((1, -1)):
            out.append((s, 0, x_send.at[par, k], x_recv.at[par, k]))
        for k, s in enumerate((1, -1)):
            out.append((0, s, y_send.at[par, k], y_recv.at[par, k]))
        for k, i in enumerate(CORNERS):
            out.append((LATTICE[i][0], LATTICE[i][1], c_send.at[par, k], c_recv.at[par, k]))
        return [m + (n,) for n, m in enumerate(out)]

    def remote(par, dx, dy, src, dst, n):
        return pltpu.make_async_remote_copy(
            src_ref=src,
            dst_ref=dst,
            send_sem=send_sem.at[par, n],
            recv_sem=recv_sem.at[par, n],
            device_id=(gx + dx, gy + dy),
            device_id_type=MESH,
        )

    def row_copy(par, j, slot):
        return pltpu.make_async_remote_copy(
            src_ref=s_send.at[par],
            dst_ref=s_recv.at[par, slot],
            send_sem=send_sem.at[par, 7 + j],
            recv_sem=recv_sem.at[par, 7 + j],
            device_id=(gx, lax.rem(gy + j, n_gy)),
            device_id_type=MESH,
        )

    def send_all(par):
        order = messages(par)
        for dx, dy, src, dst, n in order[2:]:
            pl.when(inside(dx, dy))(lambda: remote(par, dx, dy, src, dst, n).start())
        for j in range(1, n_gy):
            row_copy(par, j, gy).start()
        for dx, dy, src, dst, n in order[:2]:
            pl.when(inside(dx, dy))(lambda: remote(par, dx, dy, src, dst, n).start())

    def wait_all(par):
        for j in range(1, n_gy):
            row_copy(par, j, lax.rem(gy - j + n_gy, n_gy)).wait_recv()
        for dx, dy, src, dst, n in messages(par):
            pl.when(inside(-dx, -dy))(
                lambda: remote(par, dx, dy, src, dst, n).wait_recv()
            )

    def wait_sent(par):
        for j in range(1, n_gy):
            row_copy(par, j, gy).wait_send()
        for dx, dy, src, dst, n in messages(par):
            pl.when(inside(dx, dy))(lambda: remote(par, dx, dy, src, dst, n).wait_send())

    sublane = lax.broadcasted_iota(jnp.int32, (size_y, size_z), 0)
    lane = lax.broadcasted_iota(jnp.int32, (size_y, size_z), 1)

    def put(par, i, x, value):
        sx, sy, sz = LATTICE[i]
        if sz:
            value = pltpu.roll(value, sz % size_z, 1)
        if sy:
            value = pltpu.roll(value, sy % size_y, 0)
        rolled_ref[par, i, x] = value
        edge = size_x - 1 if sx > 0 else 0
        if sx and x == edge:
            side = 0 if sx > 0 else 1
            x_send[par, side, X_DIRS[sx].index(i)] = value
        if sy:
            side, row = (0, 0) if sy > 0 else (1, size_y - 1)
            line = value[row : row + 1, :]
            at = Y_DIRS[sy].index(i) * size_x + x
            y_send[par, side, at : at + 1, :] = line
            if sx and x == edge:
                c_send[par, CORNERS.index(i)] = line

    def pull(old, rx, i, x):
        sx, sy, sz = LATTICE[i]
        at = x - sx
        crossed = at < 0 or at >= size_x
        if crossed:
            value = x_recv[rx, 0 if sx > 0 else 1, X_DIRS[sx].index(i)]
        else:
            value = rolled_ref[old, i, at]
        if sy:
            side, row = (0, 0) if sy > 0 else (1, size_y - 1)
            if crossed:
                line = c_recv[rx, CORNERS.index(i)]
            else:
                slot = Y_DIRS[sy].index(i) * size_x + at
                line = y_recv[rx, side, slot : slot + 1, :]
            value = jnp.where(sublane == row, line, value)
        return value

    def total_rows(par):
        total = s_send[par]
        for j in range(n_gy):
            total = total + s_recv[par, j]
        return total

    def drive_tiles(radius_row):
        drive_row = (DRIVE_SCALE * radius_row) * radius_row
        return [
            jnp.sum(onehot_ref[x] * drive_row, axis=1, keepdims=True) for x in range(size_x)
        ]

    def relax(par, x, pops, rho, vel, drive):
        keep = 0.0 if pops is None else 1.0 - RELAX_RATE
        rate = 1.0 if pops is None else RELAX_RATE
        ux, uy, uz = vel
        speed = ux * ux + uy * uy + uz * uz
        rel = rate * rho
        level = rel - (1.5 * speed) * rel
        push = [(3.0 * rel) * u for u in vel]
        push[2] = push[2] + (3.0 * drive) * rho
        posts = [None] * 19
        rest = WEIGHTS[0] * level
        posts[0] = rest if pops is None else keep * pops[0] + rest
        for i in range(1, 19, 2):
            step = LATTICE[i]
            proj = None
            odd = None
            for comp in range(3):
                if step[comp] == 0:
                    continue
                if proj is None:
                    proj, odd = vel[comp], push[comp]
                elif step[comp] > 0:
                    proj, odd = proj + vel[comp], odd + push[comp]
                else:
                    proj, odd = proj - vel[comp], odd - push[comp]
            even = level + (4.5 * rel) * (proj * proj)
            for k, value in ((i, even + odd), (i + 1, even - odd)):
                value = WEIGHTS[i] * value
                posts[k] = value if pops is None else keep * pops[k] + value
        for i in range(19):
            post_ref[par, i, x] = posts[i]
            if i:
                put(par, i, x, posts[i])
        return speed

    def spread(x, speed):
        term = jnp.sum(links_ref[x] * speed, axis=1, keepdims=True)
        return onehot_ref[x] * term

    def gathered(old, rx, x, fl):
        pops = [post_ref[old, 0, x]]
        for i in range(1, 19):
            moved = pull(old, rx, i, x)
            pops.append(
                jnp.where(open_ref[i, x] > 0.0, moved, post_ref[old, reverse_of(i), x])
            )
        rho = pops[0]
        for i in range(1, 19):
            rho = rho + pops[i]
        momentum = []
        for comp in range(3):
            up = functools.reduce(
                lambda a, b: a + b, [pops[i] for i in range(19) if LATTICE[i][comp] == 1]
            )
            down = functools.reduce(
                lambda a, b: a + b, [pops[i] for i in range(19) if LATTICE[i][comp] == -1]
            )
            momentum.append(up - down)
        inverse = 1.0 / (rho + 1.0 - fl)
        return pops, rho, [m * inverse for m in momentum]

    def respond(par):
        total = total_rows(par)
        return row_ref[0:1, :] * (
            0.6
            + 0.8 * jnp.tanh(100.0 * total[0:1, :] / jnp.maximum(total[1:2, :], 1.0))
        )

    x_recv[...] = jnp.zeros_like(x_recv)
    y_recv[...] = jnp.zeros_like(y_recv)
    c_recv[...] = jnp.zeros_like(c_recv)
    s_recv[...] = jnp.zeros_like(s_recv)

    barrier = pltpu.get_barrier_semaphore()
    expected = jnp.int32(n_gy - 1)
    for j in range(1, n_gy):
        pl.semaphore_signal(
            barrier, inc=1, device_id=(gx, lax.rem(gy + j, n_gy)), device_id_type=MESH
        )
    for dx in (-1, 1):
        for dy in (-1, 0, 1):
            ok = inside(dx, dy)
            pl.when(ok)(
                lambda: pl.semaphore_signal(
                    barrier, inc=1, device_id=(gx + dx, gy + dy), device_id_type=MESH
                )
            )
            expected = expected + ok.astype(jnp.int32)

    shares = [mask_ref[x].astype(f32) for x in range(size_x)]
    for x in range(size_x):
        for i in range(1, 19):
            put(0, i, x, shares[x])
    wide = lax.broadcasted_iota(jnp.int32, (1, lanes), 1)
    own_row = jnp.zeros((1, lanes), f32)
    for j in range(units_own):
        own_row = jnp.where(wide == gy * units_own + j, base_ref[j], own_row)
    s_send[0, 0:1, :] = own_row
    s_send[0, 1:2, :] = jnp.zeros((1, lanes), f32)
    pl.semaphore_wait(barrier, expected)
    send_all(0)

    wide_y = lax.broadcasted_iota(jnp.int32, (size_y, lanes), 1)
    eye = lax.broadcasted_iota(jnp.int32, (size_y, size_y), 0) == lax.broadcasted_iota(
        jnp.int32, (size_y, size_y), 1
    )
    for x in range(size_x):
        names = jnp.broadcast_to(unit_ref[x : x + 1, :].astype(f32), (size_y, size_y))
        names = jnp.sum(jnp.where(eye, names, 0.0), axis=1, keepdims=True)
        onehot_ref[x] = jnp.where(wide_y.astype(f32) == names, 1.0, 0.0)

    wait_all(0)
    link_part = jnp.zeros((size_y, lanes), f32)
    for x in range(size_x):
        count = jnp.full((size_y, size_z), 18.0, f32)
        for i in range(1, 19):
            sz = LATTICE[i][2]
            value = pull(0, 0, i, x)
            if sz:
                value = jnp.where(lane == (0 if sz > 0 else size_z - 1), 0.0, value)
            value = value * shares[x]
            open_ref[i, x] = value
            count = count - value
        links_ref[x] = count * shares[x]
        link_part = link_part + spread(x, 1.0)
    row_ref[...] = total_rows(0)

    drives = drive_tiles(row_ref[0:1, :])
    part = jnp.zeros((size_y, lanes), f32)
    for x in range(size_x):
        rho = density_ref[x] * shares[x]
        vel = [velocity_ref[c, x] * shares[x] for c in range(3)]
        part = part + spread(x, relax(1, x, None, rho, vel, drives[x]))
    s_send[1, 0:1, :] = jnp.sum(part, axis=0, keepdims=True)
    link_row = jnp.sum(link_part, axis=0, keepdims=True)
    s_send[1, 1:2, :] = link_row
    send_all(1)
    wait_sent(0)
    s_send[0, 1:2, :] = link_row

    def step(r, carry):
        old = lax.rem(r, 2)
        new = 1 - old
        wait_all(old)
        drives = drive_tiles(respond(old))
        part = jnp.zeros((size_y, lanes), f32)
        for x in range(size_x):
            fl = mask_ref[x].astype(f32)
            pops, rho, vel = gathered(old, old, x, fl)
            part = part + spread(x, relax(new, x, pops, rho, vel, drives[x]))
        s_send[new, 0:1, :] = jnp.sum(part, axis=0, keepdims=True)
        send_all(new)
        wait_sent(old)
        return carry

    lax.fori_loop(1, STEPS, step, 0)

    last = STEPS % 2
    wait_all(last)
    wait_sent(last)
    radius = respond(last)
    radius = pltpu.roll(
        jnp.broadcast_to(radius, (8, lanes)), lax.rem(lanes - gy * units_own, lanes), 1
    )
    radius_out[...] = radius[0:1, 0:units_own]
    for x in range(size_x):
        fl = mask_ref[x].astype(f32)
        pops, rho, vel = gathered(last, last, x, fl)
        density_out[x] = rho
        for comp in range(3):
            velocity_out[comp, x] = vel[comp]


def hand_over(rho, vel, radius, rho_out, vel_out, radius_out):
    rho_out[...] = rho[...]
    vel_out[...] = vel[...]
    radius_out[...] = radius[...]


def per_device(n_gx, n_gy, density, velocity, fluid_mask, unit_of_column, radius_base):
    size_x, size_y, size_z = density.shape
    units_own = radius_base.shape[0]
    lanes = -(-units_own * n_gy // 128) * 128
    f32 = jnp.float32
    tile = (size_x, size_y, size_z)
    copies = 7 + n_gy + 1
    vmem = pl.BlockSpec(memory_space=pltpu.VMEM)
    smem = pl.BlockSpec(memory_space=pltpu.SMEM)
    rho, vel, radius = pl.pallas_call(
        functools.partial(kernel, n_gx, n_gy),
        out_shape=(
            jax.ShapeDtypeStruct(density.shape, f32),
            jax.ShapeDtypeStruct(velocity.shape, f32),
            jax.ShapeDtypeStruct((1, units_own), f32),
        ),
        in_specs=[vmem, vmem, vmem, vmem, smem],
        out_specs=(vmem, vmem, vmem),
        scratch_shapes=[
            pltpu.VMEM((19,) + tile, f32),
            pltpu.VMEM(tile, f32),
            pltpu.VMEM((size_x, size_y, lanes), f32),
            pltpu.VMEM((2, lanes), f32),
            pltpu.VMEM((2, 19) + tile, f32),
            pltpu.VMEM((2, 19) + tile, f32),
            pltpu.VMEM((2, 2, 5, size_y, size_z), f32),
            pltpu.VMEM((2, 2, 5 * size_x, size_z), f32),
            pltpu.VMEM((2, 4, 1, size_z), f32),
            pltpu.VMEM((2, 2, lanes), f32),
            pltpu.VMEM((2, 2, 5, size_y, size_z), f32),
            pltpu.VMEM((2, 2, 5 * size_x, size_z), f32),
            pltpu.VMEM((2, 4, 1, size_z), f32),
            pltpu.VMEM((2, n_gy, 2, lanes), f32),
            pltpu.SemaphoreType.DMA((2, copies)),
            pltpu.SemaphoreType.DMA((2, copies)),
        ],
        compiler_params=pltpu.CompilerParams(collective_id=0, has_side_effects=True),
    )(density, velocity, fluid_mask, unit_of_column, radius_base)
    rho, vel, radius = pl.pallas_call(
        hand_over,
        out_shape=(
            jax.ShapeDtypeStruct(density.shape, f32),
            jax.ShapeDtypeStruct(velocity.shape, f32),
            jax.ShapeDtypeStruct((1, units_own), f32),
        ),
        in_specs=[vmem, vmem, vmem],
        out_specs=(vmem, vmem, vmem),
    )(rho, vel, radius)
    return rho, vel, radius.reshape(units_own)


def solution(mesh):
    return jax.shard_map(
        functools.partial(per_device, mesh.shape["gx"], mesh.shape["gy"]),
        mesh=mesh,
        in_specs=(
            P("gx", "gy", None),
            P(None, "gx", "gy", None),
            P("gx", "gy", None),
            P("gx", "gy"),
            P(("gx", "gy")),
        ),
        out_specs=(P("gx", "gy", None), P(None, "gx", "gy", None), P(("gx", "gy"))),
        check_vma=False,
    )
```
